256 devices in a mesh: segment: 32 (over z, x), col: 8 (over y, core).
Axes of the slice: x: 4, y: 4, z: 8, core: 2. Of those that a mesh axis runs over, the one named last changes fastest.
Arguments:
- acts: float32 [128, 65536], P(None, 'col'), may hold values from 0 to 8
- tiles: bfloat16 [32, 768, 128, 128], P('segment', 'col'), may hold values from -0.625 to 0.625
- tile_row: int32 [32, 768], P('segment', 'col'), may hold values from 0 to 511, as said below
- tile_col: int32 [32, 768], P('segment', 'col'), may hold values from 0 to 63
- tile_count: int32 [32, 8], P('segment', 'col'), may hold values from 72 to 96, as said below
- bias: float32 [32, 65536], P('segment', 'col'), may hold values from -1 to 1
Outputs:
- final_acts: float32 [128, 65536], P('segment', 'col')
The draws below stay inside these ranges and needn't reach their ends.
Inputs may be any that keep to these rules, and one draw needn't show every extreme that they name: `tile_row`: a slot of column shard c reads an input block from c * 64 - 32 to (c + 1) * 64 + 31, within the layer; in every layer each shard has valid slots at both ends of that band. `tile_count`: in every layer some column shard has all 96 slots valid; the valid slots of a shard are its first ones.
All inputs are finite; a program needn't handle non-finite values.
Results may differ from the reference program's by a relative error of at most 0.0006.
Values sent between devices are 32-bit elements; how exact they have to be, the bound alone decides.
A program may use at most 64 MiB of HBM per device.

```python
import jax
import jax.numpy as jnp
from jax import lax

TB = 128
COLB = 64
REACH = 32
TILE_CAP = 96
SECTIONS = 32
NBLK = 512
N = 65536
ROWS = 128
N_COL = 8


def draw_tile_row(key, part):
    key = jax.random.fold_in(key, 11)
    shards = NBLK // COLB
    first_key, second_key, third_key = jax.random.split(key, 3)
    slots = jnp.arange(shards * TILE_CAP, dtype=jnp.int32)
    owner = (slots // TILE_CAP)[None, :]
    within = (slots % TILE_CAP)[None, :]
    lowest = jnp.maximum(owner * COLB - REACH, 0)
    highest = jnp.minimum((owner + 1) * COLB + REACH, NBLK)
    lowest = jnp.broadcast_to(lowest, (SECTIONS, shards * TILE_CAP))
    highest = jnp.broadcast_to(highest, (SECTIONS, shards * TILE_CAP))
    picked = jax.random.randint(first_key, (SECTIONS, shards * TILE_CAP), lowest, highest)
    head = 3 * TILE_CAP // 4
    first_slot = jax.random.randint(second_key, (SECTIONS, shards), 0, head)
    second_slot = (first_slot + 1 + jax.random.randint(third_key, (SECTIONS, shards), 0, head - 1)) % head
    first_slot = jnp.repeat(first_slot, TILE_CAP, axis=1)
    second_slot = jnp.repeat(second_slot, TILE_CAP, axis=1)
    picked = jnp.where(within == first_slot, lowest, picked)
    picked = jnp.where(within == second_slot, highest - 1, picked)
    return picked.astype(jnp.int32)


def draw_tile_count(key, part):
    key = jax.random.fold_in(key, 12)
    shards = NBLK // COLB
    first_key, second_key = jax.random.split(key)
    counts = jax.random.randint(first_key, (SECTIONS, shards), 3 * TILE_CAP // 4, TILE_CAP + 1)
    fullest = jax.random.randint(second_key, (SECTIONS, 1), 0, shards)
    counts = jnp.where(jnp.arange(shards, dtype=jnp.int32)[None, :] == fullest, TILE_CAP, counts)
    return counts.astype(jnp.int32)


def set_ends(entries, stream_key, low, top_value):
    extent = entries.shape
    place = [jax.random.randint(jax.random.fold_in(stream_key, axis), (), 0, extent[axis]) for axis in range(len(extent))]
    entries = entries.at[tuple(place)].set(low)
    longest = extent.index(max(extent))
    place[longest] = (place[longest] + 1) % extent[longest]
    return entries.at[tuple(place)].set(top_value)


def block_scale(stream_key, dims, cuts, least, largest):
    loudness, own = 1.0, jax.random.fold_in(stream_key, 6)
    for dim, parts in cuts:
        draws = jnp.exp(jax.random.uniform(jax.random.fold_in(own, dim), (parts,), jnp.float32, least / len(cuts), largest / len(cuts)))
        loudness = loudness * jnp.repeat(draws, dims[dim] // parts).reshape([-1 if axis == dim else 1 for axis in range(len(dims))])
    return loudness


def normal_values(stream_key, shape, width, bound, cuts=(), kind=jnp.bfloat16):
    drawn = width * jax.random.normal(stream_key, shape, jnp.float32)
    if cuts:
        drawn = drawn * block_scale(stream_key, shape, cuts, -0.22, 0.18)
    return jnp.clip(drawn, -bound, bound).astype(kind)


def setup_inputs(seed: int = 0) -> dict:
    key_list = jax.random.split(jax.random.key(seed), 7)
    acts = jnp.clip(8.0 * jax.random.uniform(key_list[0], (ROWS, N), jnp.float32) ** block_scale(key_list[0], (ROWS, N), ((1, 8),), -0.2, 0.2), 0.0, 8.0)
    tiles = normal_values(key_list[1], (SECTIONS, N_COL * TILE_CAP, TB, TB), (7 * TILE_CAP * TB // (16 * COLB)) ** -0.5, 0.625, ((0, 32), (1, 8)))
    tile_row = draw_tile_row(jax.random.fold_in(key_list[6], 71), 0)
    tile_col = set_ends(jax.random.randint(key_list[3], (SECTIONS, N_COL * TILE_CAP), 0, COLB), jax.random.fold_in(key_list[3], 1), 0, COLB - 1).astype(jnp.int32)
    tile_count = draw_tile_count(jax.random.fold_in(key_list[6], 71), 0)
    bias = jnp.clip(jax.random.uniform(key_list[5], (SECTIONS, N), jnp.float32, -1.0, 1.0) * block_scale(key_list[5], (SECTIONS, N), ((0, 32), (1, 8)), -0.4, 0.0), -1.0, 1.0)
    return dict(acts=acts, tiles=tiles, tile_row=tile_row, tile_col=tile_col, tile_count=tile_count, bias=bias)


def reference(acts, tiles, tile_row, tile_col, tile_count, bias):
    shards = NBLK // COLB
    slots = jnp.arange(shards * TILE_CAP, dtype=jnp.int32)
    owner = slots // TILE_CAP
    within = slots % TILE_CAP

    def layer(state, inputs):
        weights, rows, cols, counts, shift = inputs
        valid = (within < counts[owner]).astype(jnp.float32)
        blocks = state.reshape(ROWS, NBLK, TB)[:, rows, :].astype(jnp.float32)
        partial_sum = jnp.einsum("rsk,skj->rsj", blocks, weights.astype(jnp.float32), precision=lax.Precision.HIGHEST)
        partial_sum = partial_sum * valid[None, :, None]
        target = (owner * COLB + cols).astype(jnp.int32)
        total = jnp.zeros((ROWS, NBLK, TB), jnp.float32).at[:, target, :].add(partial_sum)
        total = total.reshape(ROWS, N) + shift[None, :]
        return jnp.clip(total, 0.0, 32.0).astype(jnp.float32), None

    final_acts, unused = lax.scan(layer, acts.astype(jnp.float32), (tiles, tile_row, tile_col, tile_count, bias))
    return final_acts
```

```python
import functools

import jax
import jax.numpy as jnp
from jax import lax
from jax.experimental import pallas as pl
from jax.experimental.pallas import tpu as pltpu
from jax.sharding import PartitionSpec as P

REACH = 32
SEGS = 32
COLS = 8
OWN = 64
EXT = OWN + 2 * REACH
CAP = 96
TB = 128
ROWS = 128
R = 2
MICRO = ROWS // R
PARTS = 3
PAD = 8 if PARTS * R <= 8 else 16
FIN = ROWS // SEGS // R
MESH = pl.DeviceIdType.MESH
F32 = jnp.float32
BF16 = jnp.bfloat16


def kernel(
    order_ref, row_ref, same_ref, last_ref, acts_hbm, tiles_hbm, bias_ref, out_ref,
    acts, raw, weights, ext, held, picked, sums, fin,
    own_sem, halo_sem, fin_sem, send_sem, local_sem,
):
    seg = lax.axis_index("segment")
    col = lax.axis_index("col")
    is_first = seg == 0
    is_last = seg == SEGS - 1
    far = lax.rem(col, 2)
    near = 1 - far
    far_col = col - 1 + 2 * far
    near_col = col - 1 + 2 * near
    has_far = (far_col >= 0) & (far_col < COLS)

    tiles_copy = pltpu.make_async_copy(tiles_hbm, raw, local_sem.at[0])
    tiles_copy.start()
    acts_copy = pltpu.make_async_copy(acts_hbm, acts, local_sem.at[1])

    @pl.when(is_first)
    def _():
        acts_copy.start()

    barrier = pltpu.get_barrier_semaphore()

    def greet(s, c):
        pl.semaphore_signal(barrier, inc=1, device_id=(s, c), device_id_type=MESH)

    greet(seg, near_col)
    pl.when(has_far)(lambda: greet(seg, far_col))
    pl.when(seg > 0)(lambda: greet(seg - 1, col))
    pl.when(seg < SEGS - 1)(lambda: greet(SEGS - 1, col))

    tiles_copy.wait()
    for j in range(CAP):
        weights[j] = raw[order_ref[j]]
    sums[CAP] = jnp.zeros((PAD, TB), F32)

    pl.when(is_first)(lambda: acts_copy.wait())

    peers = 1 + has_far.astype(jnp.int32) + jnp.where(is_last, SEGS - 1, 1)
    pl.semaphore_wait(barrier, peers)

    def own_part(m, half):
        return ext.at[m, pl.ds(REACH + REACH * half, REACH)]

    def forward(m, half, target, sem):
        pltpu.make_async_remote_copy(
            src_ref=own_part(m, half),
            dst_ref=ext.at[m, pl.ds((EXT - REACH) * (1 - half), REACH)],
            send_sem=send_sem.at[sem],
            recv_sem=halo_sem.at[m, 1 - half],
            device_id=(seg, target),
            device_id_type=MESH,
        ).start()

    def await_own(m, half):
        part = own_part(m, half)
        pltpu.make_async_copy(part, part, own_sem.at[m, half]).wait()

    def receive(m):
        @pl.when(is_first)
        def _():
            for place in range(8 // R):
                @pl.when(lax.rem(m, 8 // R) == place)
                def _():
                    for b in range(OWN):
                        ext[m, REACH + b] = acts[
                            m // (8 // R), place * R:(place + 1) * R, b * TB:(b + 1) * TB
                        ]

        @pl.when(jnp.logical_not(is_first))
        def _():
            await_own(m, far)

        pl.when(has_far)(lambda: forward(m, far, far_col, 1))

        @pl.when(jnp.logical_not(is_first))
        def _():
            await_own(m, near)

        forward(m, near, near_col, 2)

    def await_halo(m):
        def one(side):
            part = ext.at[m, pl.ds((EXT - REACH) * side, REACH)]
            pltpu.make_async_copy(part, part, halo_sem.at[m, side]).wait()

        one(near)
        pl.when(has_far)(lambda: one(far))

    sub = lax.broadcasted_iota(jnp.int32, (PAD, TB), 0)

    def split(x):
        x = jnp.concatenate([x] * (PAD // R), axis=0)
        high = x.astype(BF16).astype(F32)
        rest = x - high
        middle = rest.astype(BF16).astype(F32)
        low = rest - middle
        parts = jnp.where(sub < R, high, jnp.where(sub < 2 * R, middle, jnp.where(sub < 3 * R, low, 0.0)))
        return parts.astype(BF16)

    def compute(m):
        picked[...] = ext[m]
        run = jnp.zeros((PAD, TB), F32)
        for j in range(0, CAP, 2):
            a = split(picked[row_ref[j]])
            b = split(picked[row_ref[j + 1]])
            zero = jnp.zeros_like(a)
            left = jnp.concatenate(
                [jnp.concatenate([a, zero], 1), jnp.concatenate([zero, b], 1)], 0
            )
            right = weights[j:j + 2].reshape(2 * TB, TB)
            prod = jnp.dot(left, right, preferred_element_type=F32)
            run = jnp.where(same_ref[j] != 0, run, 0.0) + prod[:PAD]
            sums[j] = run
            run = jnp.where(same_ref[j + 1] != 0, run, 0.0) + prod[PAD:]
            sums[j + 1] = run
        for c in range(OWN):
            v = sums[last_ref[c]]
            total = v[0:R] + v[R:2 * R]
            if PARTS == 3:
                total = total + v[2 * R:3 * R]
            held[m, c] = jnp.clip(total + bias_ref[0:1, c * TB:(c + 1) * TB], 0.0, 32.0)

    def send(m):
        @pl.when(jnp.logical_not(is_last))
        def _():
            for half in (far, near):
                pltpu.make_async_remote_copy(
                    src_ref=held.at[m, pl.ds(REACH * half, REACH)],
                    dst_ref=own_part(m, half),
                    send_sem=send_sem.at[0],
                    recv_sem=own_sem.at[m, half],
                    device_id=(seg + 1, col),
                    device_id_type=MESH,
                ).start()

        target = m // FIN
        place = lax.rem(m, FIN)

        @pl.when(is_last & (target < SEGS - 1))
        def _():
            pltpu.make_async_remote_copy(
                src_ref=held.at[m],
                dst_ref=fin.at[place],
                send_sem=send_sem.at[0],
                recv_sem=fin_sem.at[place],
                device_id=(target, col),
                device_id_type=MESH,
            ).start()

        @pl.when(is_last & (target == SEGS - 1))
        def _():
            pltpu.make_async_copy(held.at[m], fin.at[place], fin_sem.at[place]).start()

    receive(0)

    def step(m, carry):
        await_halo(m)
        pl.when(m + 1 < MICRO)(lambda: receive(m + 1))
        compute(m)
        send(m)
        return carry

    lax.fori_loop(0, MICRO, step, 0)

    for place in range(FIN):
        pltpu.make_async_copy(fin.at[place], fin.at[place], fin_sem.at[place]).wait()
        for c in range(OWN):
            out_ref[place * R:(place + 1) * R, c * TB:(c + 1) * TB] = fin[place, c]

    def drain(part, sem):
        pltpu.make_async_copy(part, part, send_sem.at[sem]).wait()

    @pl.when(is_last)
    def _():
        drain(held.at[pl.ds(0, MICRO - FIN)], 0)

    @pl.when(jnp.logical_not(is_last))
    def _():
        drain(held, 0)

    pl.when(has_far)(lambda: drain(ext.at[:, pl.ds(0, REACH)], 1))
    drain(ext.at[:, pl.ds(0, REACH)], 2)


def prepare(tile_row, tile_col, tile_count):
    column = lax.axis_index("col")
    slots = jnp.arange(CAP, dtype=jnp.int32)
    valid = slots < tile_count[0, 0]
    row = jnp.where(valid, tile_row[0] - column * OWN + REACH, REACH)
    target = jnp.where(valid, tile_col[0], OWN)
    key = target * CAP + slots
    rank = jnp.sum((key[None, :] < key[:, None]).astype(jnp.int32), axis=1)
    place = rank[None, :] == slots[:, None]

    def ordered(values):
        return jnp.sum(jnp.where(place, values[None, :], 0), axis=1)

    order, row, target_sorted = ordered(slots), ordered(row), ordered(target)
    former = jnp.concatenate([jnp.full((1,), -1, jnp.int32), target_sorted[:-1]])
    same = (target_sorted == former).astype(jnp.int32)
    blocks = jnp.arange(OWN, dtype=jnp.int32)
    count = jnp.sum((target[None, :] == blocks[:, None]).astype(jnp.int32), axis=1)
    upto = jnp.sum((target[None, :] <= blocks[:, None]).astype(jnp.int32), axis=1)
    last = jnp.where(count > 0, upto - 1, CAP)
    return order, row, same, last


def local(acts, tiles, tile_row, tile_col, tile_count, bias):
    tables = prepare(tile_row, tile_col, tile_count)
    smem = pl.BlockSpec(memory_space=pltpu.SMEM)
    vmem = pl.BlockSpec(memory_space=pltpu.VMEM)
    hbm = pl.BlockSpec(memory_space=pl.ANY)
    dma = pltpu.SemaphoreType.DMA
    return pl.pallas_call(
        kernel,
        out_shape=jax.ShapeDtypeStruct((ROWS // SEGS, OWN * TB), F32),
        in_specs=[smem, smem, smem, smem, hbm, hbm, vmem],
        out_specs=vmem,
        scratch_shapes=[
            pltpu.VMEM((ROWS // 8, 8, OWN * TB), F32),
            pltpu.VMEM((CAP, TB, TB), BF16),
            pltpu.VMEM((CAP, TB, TB), BF16),
            pltpu.VMEM((MICRO, EXT, R, TB), F32),
            pltpu.VMEM((MICRO, OWN, R, TB), F32),
            pltpu.VMEM((EXT, R, TB), F32),
            pltpu.VMEM((CAP + 1, PAD, TB), F32),
            pltpu.VMEM((FIN, OWN, R, TB), F32),
            dma((MICRO, 2)),
            dma((MICRO, 2)),
            dma((FIN,)),
            dma((3,)),
            dma((2,)),
        ],
        compiler_params=pltpu.CompilerParams(
            collective_id=0, has_side_effects=True, vmem_limit_bytes=48 << 20
        ),
        cost_estimate=pl.CostEstimate(
            flops=2 * ROWS * CAP * TB * TB, bytes_accessed=8 << 20, transcendentals=0
        ),
    )(*tables, acts.reshape(ROWS // 8, 8, OWN * TB), tiles[0], bias)


def solution(mesh):
    placed = (
        P(None, "col"),
        P("segment", "col", None, None),
        P("segment", "col"),
        P("segment", "col"),
        P("segment", "col"),
        P("segment", "col"),
    )
    return jax.shard_map(
        local, mesh=mesh, in_specs=placed, out_specs=P("segment", "col"), check_vma=False
    )
```

```python
import functools

import jax
import jax.numpy as jnp
from jax import lax
from jax.experimental import pallas as pl
from jax.experimental.pallas import tpu as pltpu
from jax.sharding import PartitionSpec as P

REACH = 32
SEGS = 32
COLS = 8
OWN = 64
EXT = OWN + 2 * REACH
CAP = 96
TB = 128
ROWS = 128
R = 1
MICRO = ROWS // R
PARTS = 3
PAD = 8 if PARTS * R <= 8 else 16
FIN = ROWS // SEGS // R
RELAY = True
AHEAD = 8 // R
MESH = pl.DeviceIdType.MESH
F32 = jnp.float32
BF16 = jnp.bfloat16


def kernel(
    order_ref, row_ref, same_ref, last_ref, acts_hbm, tiles_hbm, bias_ref, out_ref,
    acts, raw, weights, ext, held, picked, sums, fin,
    own_sem, halo_sem, fin_sem, send_sem, local_sem,
):
    seg = lax.axis_index("segment")
    col = lax.axis_index("col")
    is_first = seg == 0
    is_last = seg == SEGS - 1
    far = lax.rem(col, 2)
    near = 1 - far
    far_col = col - 1 + 2 * far
    near_col = col - 1 + 2 * near
    has_far = (far_col >= 0) & (far_col < COLS)

    tiles_copy = pltpu.make_async_copy(tiles_hbm, raw, local_sem.at[0])
    tiles_copy.start()
    acts_copy = pltpu.make_async_copy(acts_hbm, acts, local_sem.at[1])

    @pl.when(is_first)
    def _():
        acts_copy.start()

    barrier = pltpu.get_barrier_semaphore()

    def greet(s, c):
        pl.semaphore_signal(barrier, inc=1, device_id=(s, c), device_id_type=MESH)

    @pl.when(seg > 0)
    def _():
        greet(seg - 1, col)
        if not RELAY:
            greet(seg - 1, near_col)
        pl.when(has_far)(lambda: greet(seg - 1, far_col))

    @pl.when(is_first)
    def _():
        pl.when(has_far)(lambda: greet(seg, far_col))
        if not RELAY:
            greet(seg, near_col)

    if RELAY:
        greet(seg, near_col)
    pl.when(seg < SEGS - 1)(lambda: greet(SEGS - 1, col))

    tiles_copy.wait()
    for j in range(CAP):
        weights[j] = raw[order_ref[j]]
    sums[CAP] = jnp.zeros((PAD, TB), F32)

    pl.when(is_first)(lambda: acts_copy.wait())

    reach = has_far.astype(jnp.int32)
    if RELAY:
        peers = 1 + jnp.where(is_last, SEGS - 1, 1 + reach + jnp.where(is_first, reach, 0))
    else:
        peers = jnp.where(is_last, SEGS - 1, 2 + reach + jnp.where(is_first, 1 + reach, 0))
    pl.semaphore_wait(barrier, peers)

    def own_part(m, half):
        return ext.at[m, pl.ds(REACH + REACH * half, REACH)]

    def rim_part(m, side):
        return ext.at[m, pl.ds((EXT - REACH) * side, REACH)]

    def push(source, target, landing, sent, landed):
        pltpu.make_async_remote_copy(
            src_ref=source,
            dst_ref=landing,
            send_sem=send_sem.at[sent],
            recv_sem=landed,
            device_id=target,
            device_id_type=MESH,
        ).start()

    def push_rim(source, m, half, target, sent):
        push(source, target, rim_part(m, 1 - half), sent, halo_sem.at[m, 1 - half])

    def await_own(m, half):
        part = own_part(m, half)
        pltpu.make_async_copy(part, part, own_sem.at[m, half]).wait()

    def load_first(m):
        for place in range(8 // R):
            @pl.when(lax.rem(m, 8 // R) == place)
            def _():
                for b in range(OWN):
                    ext[m, REACH + b] = acts[
                        m // (8 // R), place * R:(place + 1) * R, b * TB:(b + 1) * TB
                    ]

        pl.when(has_far)(lambda: push_rim(own_part(m, far), m, far, (seg, far_col), 3))
        push_rim(own_part(m, near), m, near, (seg, near_col), 4)

    def relay(m):
        await_own(m, near)
        push_rim(own_part(m, near), m, near, (seg, near_col), 2)

    def await_input(m):
        @pl.when(jnp.logical_not(is_first))
        def _():
            if not RELAY:
                await_own(m, near)
            await_own(m, far)

        def one(side):
            part = rim_part(m, side)
            pltpu.make_async_copy(part, part, halo_sem.at[m, side]).wait()

        one(near)
        pl.when(has_far)(lambda: one(far))

    sub = lax.broadcasted_iota(jnp.int32, (PAD, TB), 0)

    def split(x):
        x = jnp.concatenate([x] * (PAD // R), axis=0)
        high = x.astype(BF16).astype(F32)
        rest = x - high
        middle = rest.astype(BF16).astype(F32)
        low = rest - middle
        parts = jnp.where(sub < R, high, jnp.where(sub < 2 * R, middle, jnp.where(sub < 3 * R, low, 0.0)))
        return parts.astype(BF16)

    def compute(m):
        picked[...] = ext[m]
        run = jnp.zeros((PAD, TB), F32)
        for j in range(0, CAP, 2):
            a = split(picked[row_ref[j]])
            b = split(picked[row_ref[j + 1]])
            zero = jnp.zeros_like(a)
            left = jnp.concatenate(
                [jnp.concatenate([a, zero], 1), jnp.concatenate([zero, b], 1)], 0
            )
            right = weights[j:j + 2].reshape(2 * TB, TB)
            prod = jnp.dot(left, right, preferred_element_type=F32)
            run = jnp.where(same_ref[j] != 0, run, 0.0) + prod[:PAD]
            sums[j] = run
            run = jnp.where(same_ref[j + 1] != 0, run, 0.0) + prod[PAD:]
            sums[j + 1] = run
        for c in range(OWN):
            v = sums[last_ref[c]]
            total = v[0:R] + v[R:2 * R]
            if PARTS == 3:
                total = total + v[2 * R:3 * R]
            held[m, c] = jnp.clip(total + bias_ref[0:1, c * TB:(c + 1) * TB], 0.0, 32.0)

    def send(m):
        @pl.when(jnp.logical_not(is_last))
        def _():
            def half_of(half):
                return held.at[m, pl.ds(REACH * half, REACH)]

            def push_own(half):
                push(half_of(half), (seg + 1, col), own_part(m, half), 0, own_sem.at[m, half])

            if RELAY:
                push_own(near)
            pl.when(has_far)(lambda: push_rim(half_of(far), m, far, (seg + 1, far_col), 1))
            push_own(far)
            if not RELAY:
                push_own(near)
                push_rim(half_of(near), m, near, (seg + 1, near_col), 2)

        target = m // FIN
        place = lax.rem(m, FIN)

        @pl.when(is_last & (target < SEGS - 1))
        def _():
            pltpu.make_async_remote_copy(
                src_ref=held.at[m],
                dst_ref=fin.at[place],
                send_sem=send_sem.at[0],
                recv_sem=fin_sem.at[place],
                device_id=(target, col),
                device_id_type=MESH,
            ).start()

        @pl.when(is_last & (target == SEGS - 1))
        def _():
            pltpu.make_async_copy(held.at[m], fin.at[place], fin_sem.at[place]).start()

    @pl.when(is_first)
    def _():
        for m in range(AHEAD):
            load_first(m)

    if RELAY:
        pl.when(jnp.logical_not(is_first))(lambda: relay(0))

    def step(m, carry):
        pl.when(is_first & (m + AHEAD < MICRO))(lambda: load_first(m + AHEAD))
        if RELAY:
            pl.when(jnp.logical_not(is_first) & (m + 1 < MICRO))(lambda: relay(m + 1))
        await_input(m)
        compute(m)
        send(m)
        return carry

    lax.fori_loop(0, MICRO, step, 0)

    for place in range(FIN):
        pltpu.make_async_copy(fin.at[place], fin.at[place], fin_sem.at[place]).wait()
        for c in range(OWN):
            out_ref[place * R:(place + 1) * R, c * TB:(c + 1) * TB] = fin[place, c]

    def drain(part, sem):
        pltpu.make_async_copy(part, part, send_sem.at[sem]).wait()

    half_shape = held.at[:, pl.ds(0, REACH)]

    @pl.when(is_last)
    def _():
        drain(held.at[pl.ds(0, MICRO - FIN)], 0)

    @pl.when(jnp.logical_not(is_last))
    def _():
        drain(held, 0)
        pl.when(has_far)(lambda: drain(half_shape, 1))
        if not RELAY:
            drain(half_shape, 2)

    if RELAY:
        pl.when(jnp.logical_not(is_first))(lambda: drain(half_shape, 2))

    @pl.when(is_first)
    def _():
        pl.when(has_far)(lambda: drain(half_shape, 3))
        drain(half_shape, 4)


def prepare(tile_row, tile_col, tile_count):
    column = lax.axis_index("col")
    slots = jnp.arange(CAP, dtype=jnp.int32)
    valid = slots < tile_count[0, 0]
    row = jnp.where(valid, tile_row[0] - column * OWN + REACH, REACH)
    target = jnp.where(valid, tile_col[0], OWN)
    key = target * CAP + slots
    rank = jnp.sum((key[None, :] < key[:, None]).astype(jnp.int32), axis=1)
    place = rank[None, :] == slots[:, None]

    def ordered(values):
        return jnp.sum(jnp.where(place, values[None, :], 0), axis=1)

    order, row, target_sorted = ordered(slots), ordered(row), ordered(target)
    former = jnp.concatenate([jnp.full((1,), -1, jnp.int32), target_sorted[:-1]])
    same = (target_sorted == former).astype(jnp.int32)
    blocks = jnp.arange(OWN, dtype=jnp.int32)
    count = jnp.sum((target[None, :] == blocks[:, None]).astype(jnp.int32), axis=1)
    upto = jnp.sum((target[None, :] <= blocks[:, None]).astype(jnp.int32), axis=1)
    last = jnp.where(count > 0, upto - 1, CAP)
    return order, row, same, last


def local(acts, tiles, tile_row, tile_col, tile_count, bias):
    tables = prepare(tile_row, tile_col, tile_count)
    smem = pl.BlockSpec(memory_space=pltpu.SMEM)
    vmem = pl.BlockSpec(memory_space=pltpu.VMEM)
    hbm = pl.BlockSpec(memory_space=pl.ANY)
    dma = pltpu.SemaphoreType.DMA
    return pl.pallas_call(
        kernel,
        out_shape=jax.ShapeDtypeStruct((ROWS // SEGS, OWN * TB), F32),
        in_specs=[smem, smem, smem, smem, hbm, hbm, vmem],
        out_specs=vmem,
        scratch_shapes=[
            pltpu.VMEM((ROWS // 8, 8, OWN * TB), F32),
            pltpu.VMEM((CAP, TB, TB), BF16),
            pltpu.VMEM((CAP, TB, TB), BF16),
            pltpu.VMEM((MICRO, EXT, R, TB), F32),
            pltpu.VMEM((MICRO, OWN, R, TB), F32),
            pltpu.VMEM((EXT, R, TB), F32),
            pltpu.VMEM((CAP + 1, PAD, TB), F32),
            pltpu.VMEM((FIN, OWN, R, TB), F32),
            dma((MICRO, 2)),
            dma((MICRO, 2)),
            dma((FIN,)),
            dma((5,)),
            dma((2,)),
        ],
        compiler_params=pltpu.CompilerParams(
            collective_id=0, has_side_effects=True, vmem_limit_bytes=48 << 20
        ),
        cost_estimate=pl.CostEstimate(
            flops=2 * ROWS * CAP * TB * TB, bytes_accessed=8 << 20, transcendentals=0
        ),
    )(*tables, acts.reshape(ROWS // 8, 8, OWN * TB), tiles[0], bias)


def solution(mesh):
    placed = (
        P(None, "col"),
        P("segment", "col", None, None),
        P("segment", "col"),
        P("segment", "col"),
        P("segment", "col"),
        P("segment", "col"),
    )
    return jax.shard_map(
        local, mesh=mesh, in_specs=placed, out_specs=P("segment", "col"), check_vma=False
    )
```

```python
import functools

import jax
import jax.numpy as jnp
from jax import lax
from jax.experimental import pallas as pl
from jax.experimental.pallas import tpu as pltpu
from jax.sharding import PartitionSpec as P

REACH = 32
SEGS = 32
COLS = 8
OWN = 64
EXT = OWN + 2 * REACH
CAP = 96
TB = 128
ROWS = 128
R = 1
MICRO = ROWS // R
PAD = 8
FIN = ROWS // SEGS // R
RELAY = True
AHEAD = 8 // R
MESH = pl.DeviceIdType.MESH
F32 = jnp.float32
BF16 = jnp.bfloat16


def kernel(
    order_ref, row_ref, same_ref, last_ref, acts_hbm, tiles_hbm, bias_hbm, out_ref,
    acts, raw, weights, bias, ext, held, picked, sums, ends, fin,
    own_sem, halo_sem, fin_sem, send_sem, local_sem,
):
    seg = lax.axis_index("segment")
    col = lax.axis_index("col")
    is_first = seg == 0
    is_last = seg == SEGS - 1
    far = lax.rem(col, 2)
    near = 1 - far
    far_col = col - 1 + 2 * far
    near_col = col - 1 + 2 * near
    has_far = (far_col >= 0) & (far_col < COLS)

    tiles_copy = pltpu.make_async_copy(tiles_hbm, raw, local_sem.at[0])
    tiles_copy.start()
    bias_copy = pltpu.make_async_copy(bias_hbm, bias, local_sem.at[2])
    bias_copy.start()
    acts_copy = pltpu.make_async_copy(acts_hbm, acts, local_sem.at[1])

    @pl.when(is_first)
    def _():
        acts_copy.start()

    barrier = pltpu.get_barrier_semaphore()

    def greet(s, c):
        pl.semaphore_signal(barrier, inc=1, device_id=(s, c), device_id_type=MESH)

    @pl.when(seg > 0)
    def _():
        greet(seg - 1, col)
        if not RELAY:
            greet(seg - 1, near_col)
        pl.when(has_far)(lambda: greet(seg - 1, far_col))

    @pl.when(is_first)
    def _():
        pl.when(has_far)(lambda: greet(seg, far_col))
        if not RELAY:
            greet(seg, near_col)

    if RELAY:
        greet(seg, near_col)
    pl.when(seg < SEGS - 1)(lambda: greet(SEGS - 1, col))

    tiles_copy.wait()
    for j in range(CAP):
        weights[j] = raw[order_ref[j]]
    sums[CAP] = jnp.zeros((PAD, TB), F32)
    bias_copy.wait()

    pl.when(is_first)(lambda: acts_copy.wait())

    reach = has_far.astype(jnp.int32)
    if RELAY:
        peers = 1 + jnp.where(is_last, SEGS - 1, 1 + reach + jnp.where(is_first, reach, 0))
    else:
        peers = jnp.where(is_last, SEGS - 1, 2 + reach + jnp.where(is_first, 1 + reach, 0))
    pl.semaphore_wait(barrier, peers)

    def own_part(m, half):
        return ext.at[m, pl.ds(pl.multiple_of(REACH + REACH * half, REACH), REACH)]

    def rim_part(m, side):
        return ext.at[m, pl.ds(pl.multiple_of((EXT - REACH) * side, REACH), REACH)]

    def push(source, target, landing, sent, landed):
        pltpu.make_async_remote_copy(
            src_ref=source,
            dst_ref=landing,
            send_sem=send_sem.at[sent],
            recv_sem=landed,
            device_id=target,
            device_id_type=MESH,
        ).start()

    def push_rim(source, m, half, target, sent):
        push(source, target, rim_part(m, 1 - half), sent, halo_sem.at[m, 1 - half])

    def await_own(m, half):
        part = own_part(m, half)
        pltpu.make_async_copy(part, part, own_sem.at[m, half]).wait()

    def load_first(m):
        for place in range(8 // R):
            @pl.when(lax.rem(m, 8 // R) == place)
            def _():
                for b in range(OWN):
                    ext[m, REACH + b:REACH + b + 1] = acts[
                        m // (8 // R), place * R:(place + 1) * R, b * TB:(b + 1) * TB
                    ]

        pl.when(has_far)(lambda: push_rim(own_part(m, far), m, far, (seg, far_col), 3))
        push_rim(own_part(m, near), m, near, (seg, near_col), 4)

    def relay(m):
        await_own(m, near)
        push_rim(own_part(m, near), m, near, (seg, near_col), 2)

    def await_input(m):
        @pl.when(jnp.logical_not(is_first))
        def _():
            if not RELAY:
                await_own(m, near)
            await_own(m, far)

        def one(side):
            part = rim_part(m, side)
            pltpu.make_async_copy(part, part, halo_sem.at[m, side]).wait()

        one(near)
        pl.when(has_far)(lambda: one(far))

    sub = lax.broadcasted_iota(jnp.int32, (PAD, TB), 0)
    zero = jnp.zeros((PAD, TB), F32)

    def split(j):
        x = jnp.broadcast_to(picked[row_ref[j]].reshape(1, TB), (PAD, TB))
        high = x.astype(BF16).astype(F32)
        return jnp.where(sub < 1, high, jnp.where(sub < 2, x - high, 0.0))

    def compute(m):
        picked[...] = ext[m]
        run = zero
        for j in range(0, CAP, 2):
            upper = jnp.concatenate([split(j), zero], 0).astype(BF16)
            lower = jnp.concatenate([zero, split(j + 1)], 0).astype(BF16)
            prod = jnp.dot(
                jnp.concatenate([upper, lower], 1),
                weights[j:j + 2].reshape(2 * TB, TB),
                preferred_element_type=F32,
            )
            run = jnp.where(same_ref[j] != 0, run, 0.0) + prod[:PAD]
            sums[j] = run
            run = jnp.where(same_ref[j + 1] != 0, run, 0.0) + prod[PAD:]
            sums[j + 1] = run
        for c in range(OWN):
            ends[c * PAD:(c + 1) * PAD] = sums[last_ref[c]]
        for c in range(0, OWN, 8):
            high = ends[pl.ds(c * PAD, 8, stride=PAD), :]
            low = ends[pl.ds(c * PAD + 1, 8, stride=PAD), :]
            held[m, c:c + 8] = jnp.clip(high + low + bias[c:c + 8], 0.0, 32.0)

    def send(m):
        @pl.when(jnp.logical_not(is_last))
        def _():
            def half_of(half):
                return held.at[m, pl.ds(pl.multiple_of(REACH * half, REACH), REACH)]

            def push_own(half):
                push(half_of(half), (seg + 1, col), own_part(m, half), 0, own_sem.at[m, half])

            if RELAY:
                push_own(near)
            pl.when(has_far)(lambda: push_rim(half_of(far), m, far, (seg + 1, far_col), 1))
            push_own(far)
            if not RELAY:
                push_own(near)
                push_rim(half_of(near), m, near, (seg + 1, near_col), 2)

        target = m // FIN
        place = lax.rem(m, FIN)

        @pl.when(is_last & (target < SEGS - 1))
        def _():
            pltpu.make_async_remote_copy(
                src_ref=held.at[m],
                dst_ref=fin.at[place],
                send_sem=send_sem.at[0],
                recv_sem=fin_sem.at[place],
                device_id=(target, col),
                device_id_type=MESH,
            ).start()

        @pl.when(is_last & (target == SEGS - 1))
        def _():
            pltpu.make_async_copy(held.at[m], fin.at[place], fin_sem.at[place]).start()

    @pl.when(is_first)
    def _():
        for m in range(AHEAD):
            load_first(m)

    if RELAY:
        pl.when(jnp.logical_not(is_first))(lambda: relay(0))

    def step(m, carry):
        pl.when(is_first & (m + AHEAD < MICRO))(lambda: load_first(m + AHEAD))
        if RELAY:
            pl.when(jnp.logical_not(is_first) & (m + 1 < MICRO))(lambda: relay(m + 1))
        await_input(m)
        compute(m)
        send(m)
        return carry

    lax.fori_loop(0, MICRO, step, 0)

    for place in range(FIN):
        pltpu.make_async_copy(fin.at[place], fin.at[place], fin_sem.at[place]).wait()
        for c in range(OWN):
            out_ref[place * R:(place + 1) * R, c * TB:(c + 1) * TB] = fin[place, c:c + 1]

    def drain(part, sem):
        pltpu.make_async_copy(part, part, send_sem.at[sem]).wait()

    half_shape = held.at[:, pl.ds(0, REACH)]

    @pl.when(is_last)
    def _():
        drain(held.at[pl.ds(0, MICRO - FIN)], 0)

    @pl.when(jnp.logical_not(is_last))
    def _():
        drain(held, 0)
        pl.when(has_far)(lambda: drain(half_shape, 1))
        if not RELAY:
            drain(half_shape, 2)

    if RELAY:
        pl.when(jnp.logical_not(is_first))(lambda: drain(half_shape, 2))

    @pl.when(is_first)
    def _():
        pl.when(has_far)(lambda: drain(half_shape, 3))
        drain(half_shape, 4)


def prepare(tile_row, tile_col, tile_count):
    column = lax.axis_index("col")
    slots = jnp.arange(CAP, dtype=jnp.int32)
    valid = slots < tile_count[0, 0]
    row = jnp.where(valid, tile_row[0] - column * OWN + REACH, REACH)
    target = jnp.where(valid, tile_col[0], OWN)
    key = target * CAP + slots
    rank = jnp.sum((key[None, :] < key[:, None]).astype(jnp.int32), axis=1)
    place = rank[None, :] == slots[:, None]

    def ordered(values):
        return jnp.sum(jnp.where(place, values[None, :], 0), axis=1)

    order, row, target_sorted = ordered(slots), ordered(row), ordered(target)
    former = jnp.concatenate([jnp.full((1,), -1, jnp.int32), target_sorted[:-1]])
    same = (target_sorted == former).astype(jnp.int32)
    blocks = jnp.arange(OWN, dtype=jnp.int32)
    count = jnp.sum((target[None, :] == blocks[:, None]).astype(jnp.int32), axis=1)
    upto = jnp.sum((target[None, :] <= blocks[:, None]).astype(jnp.int32), axis=1)
    last = jnp.where(count > 0, upto - 1, CAP)
    return order, row, same, last


def local(acts, tiles, tile_row, tile_col, tile_count, bias):
    tables = prepare(tile_row, tile_col, tile_count)
    smem = pl.BlockSpec(memory_space=pltpu.SMEM)
    vmem = pl.BlockSpec(memory_space=pltpu.VMEM)
    hbm = pl.BlockSpec(memory_space=pl.ANY)
    dma = pltpu.SemaphoreType.DMA
    return pl.pallas_call(
        kernel,
        out_shape=jax.ShapeDtypeStruct((ROWS // SEGS, OWN * TB), F32),
        in_specs=[smem, smem, smem, smem, hbm, hbm, hbm],
        out_specs=vmem,
        scratch_shapes=[
            pltpu.VMEM((ROWS // 8, 8, OWN * TB), F32),
            pltpu.VMEM((CAP, TB, TB), BF16),
            pltpu.VMEM((CAP, TB, TB), BF16),
            pltpu.VMEM((OWN, TB), F32),
            pltpu.VMEM((MICRO, EXT, TB), F32),
            pltpu.VMEM((MICRO, OWN, TB), F32),
            pltpu.VMEM((EXT, TB), F32),
            pltpu.VMEM((CAP + 1, PAD, TB), F32),
            pltpu.VMEM((OWN * PAD, TB), F32),
            pltpu.VMEM((FIN, OWN, TB), F32),
            dma((MICRO, 2)),
            dma((MICRO, 2)),
            dma((FIN,)),
            dma((5,)),
            dma((3,)),
        ],
        compiler_params=pltpu.CompilerParams(
            collective_id=0, has_side_effects=True, vmem_limit_bytes=60 << 20
        ),
        cost_estimate=pl.CostEstimate(
            flops=2 * ROWS * CAP * TB * TB, bytes_accessed=8 << 20, transcendentals=0
        ),
    )(*tables, acts.reshape(ROWS // 8, 8, OWN * TB), tiles[0], bias.reshape(OWN, TB))


def solution(mesh):
    placed = (
        P(None, "col"),
        P("segment", "col", None, None),
        P("segment", "col"),
        P("segment", "col"),
        P("segment", "col"),
        P("segment", "col"),
    )
    return jax.shard_map(
        local, mesh=mesh, in_specs=placed, out_specs=P("segment", "col"), check_vma=False
    )
```

```python
import functools

import jax
import jax.numpy as jnp
from jax import lax
from jax.experimental import pallas as pl
from jax.experimental.pallas import tpu as pltpu
from jax.sharding import PartitionSpec as P

REACH = 32
SEGS = 32
COLS = 8
OWN = 64
EXT = OWN + 2 * REACH
CAP = 96
TB = 128
ROWS = 128
R = 1
MICRO = ROWS // R
PAD = 8
FIN = ROWS // SEGS // R
RELAY = True
AHEAD = 4
MESH = pl.DeviceIdType.MESH
F32 = jnp.float32
BF16 = jnp.bfloat16


def kernel(
    order_ref, row_ref, same_ref, last_ref, acts_hbm, tiles_hbm, bias_hbm, out_ref,
    acts, raw, weights, bias, ext, held, picked, sums, ends, fin,
    own_sem, halo_sem, fin_sem, send_sem, local_sem,
):
    seg = lax.axis_index("segment")
    col = lax.axis_index("col")
    is_first = seg == 0
    is_last = seg == SEGS - 1
    far = lax.rem(col, 2)
    near = 1 - far
    far_col = col - 1 + 2 * far
    near_col = col - 1 + 2 * near
    has_far = (far_col >= 0) & (far_col < COLS)

    tiles_copy = pltpu.make_async_copy(tiles_hbm, raw, local_sem.at[0])
    tiles_copy.start()
    bias_copy = pltpu.make_async_copy(bias_hbm, bias, local_sem.at[2])
    bias_copy.start()
    acts_copy = pltpu.make_async_copy(acts_hbm, acts, local_sem.at[1])

    @pl.when(is_first)
    def _():
        acts_copy.start()

    barrier = pltpu.get_barrier_semaphore()

    def greet(s, c):
        pl.semaphore_signal(barrier, inc=1, device_id=(s, c), device_id_type=MESH)

    @pl.when(seg > 0)
    def _():
        greet(seg - 1, col)
        if not RELAY:
            greet(seg - 1, near_col)
        pl.when(has_far)(lambda: greet(seg - 1, far_col))

    @pl.when(is_first)
    def _():
        pl.when(has_far)(lambda: greet(seg, far_col))
        if not RELAY:
            greet(seg, near_col)

    if RELAY:
        greet(seg, near_col)
    pl.when(seg < SEGS - 1)(lambda: greet(SEGS - 1, col))

    pl.when(is_first)(lambda: acts_copy.wait())

    reach = has_far.astype(jnp.int32)
    if RELAY:
        peers = 1 + jnp.where(is_last, SEGS - 1, 1 + reach + jnp.where(is_first, reach, 0))
    else:
        peers = jnp.where(is_last, SEGS - 1, 2 + reach + jnp.where(is_first, 1 + reach, 0))
    pl.semaphore_wait(barrier, peers)

    def own_part(m, half):
        return ext.at[m, pl.ds(pl.multiple_of(REACH + REACH * half, REACH), REACH)]

    def rim_part(m, side):
        return ext.at[m, pl.ds(pl.multiple_of((EXT - REACH) * side, REACH), REACH)]

    def push(source, target, landing, sent, landed):
        pltpu.make_async_remote_copy(
            src_ref=source,
            dst_ref=landing,
            send_sem=send_sem.at[sent],
            recv_sem=landed,
            device_id=target,
            device_id_type=MESH,
        ).start()

    def push_rim(source, m, half, target, sent):
        push(source, target, rim_part(m, 1 - half), sent, halo_sem.at[m, 1 - half])

    def await_own(m, half):
        part = own_part(m, half)
        pltpu.make_async_copy(part, part, own_sem.at[m, half]).wait()

    def load_first(m):
        for place in range(8 // R):
            @pl.when(lax.rem(m, 8 // R) == place)
            def _():
                for b in range(OWN):
                    ext[m, REACH + b:REACH + b + 1] = acts[
                        m // (8 // R), place * R:(place + 1) * R, b * TB:(b + 1) * TB
                    ]

        pl.when(has_far)(lambda: push_rim(own_part(m, far), m, far, (seg, far_col), 3))
        push_rim(own_part(m, near), m, near, (seg, near_col), 4)

    def relay(m):
        await_own(m, near)
        push_rim(own_part(m, near), m, near, (seg, near_col), 2)

    def await_input(m):
        @pl.when(jnp.logical_not(is_first))
        def _():
            if not RELAY:
                await_own(m, near)
            await_own(m, far)

        def one(side):
            part = rim_part(m, side)
            pltpu.make_async_copy(part, part, halo_sem.at[m, side]).wait()

        one(near)
        pl.when(has_far)(lambda: one(far))

    sub = lax.broadcasted_iota(jnp.int32, (PAD, TB), 0)
    zero = jnp.zeros((PAD, TB), F32)

    def split(j):
        x = jnp.broadcast_to(picked[row_ref[j]].reshape(1, TB), (PAD, TB))
        high = x.astype(BF16).astype(F32)
        return jnp.where(sub < 1, high, jnp.where(sub < 2, x - high, 0.0))

    def compute(m):
        picked[...] = ext[m]
        run = zero
        for j in range(0, CAP, 2):
            upper = jnp.concatenate([split(j), zero], 0).astype(BF16)
            lower = jnp.concatenate([zero, split(j + 1)], 0).astype(BF16)
            prod = jnp.dot(
                jnp.concatenate([upper, lower], 1),
                weights[j:j + 2].reshape(2 * TB, TB),
                preferred_element_type=F32,
            )
            run = jnp.where(same_ref[j] != 0, run, 0.0) + prod[:PAD]
            sums[j] = run
            run = jnp.where(same_ref[j + 1] != 0, run, 0.0) + prod[PAD:]
            sums[j + 1] = run
        for c in range(OWN):
            ends[c * PAD:(c + 1) * PAD] = sums[last_ref[c]]
        for c in range(0, OWN, 8):
            high = ends[pl.ds(c * PAD, 8, stride=PAD), :]
            low = ends[pl.ds(c * PAD + 1, 8, stride=PAD), :]
            held[m, c:c + 8] = jnp.clip(high + low + bias[c:c + 8], 0.0, 32.0)

    def send(m):
        @pl.when(jnp.logical_not(is_last))
        def _():
            def half_of(half):
                return held.at[m, pl.ds(pl.multiple_of(REACH * half, REACH), REACH)]

            def push_own(half):
                push(half_of(half), (seg + 1, col), own_part(m, half), 0, own_sem.at[m, half])

            if RELAY:
                push_own(near)
            pl.when(has_far)(lambda: push_rim(half_of(far), m, far, (seg + 1, far_col), 1))
            push_own(far)
            if not RELAY:
                push_own(near)
                push_rim(half_of(near), m, near, (seg + 1, near_col), 2)

        target = m // FIN
        place = lax.rem(m, FIN)

        @pl.when(is_last & (target < SEGS - 1))
        def _():
            pltpu.make_async_remote_copy(
                src_ref=held.at[m],
                dst_ref=fin.at[place],
                send_sem=send_sem.at[0],
                recv_sem=fin_sem.at[place],
                device_id=(target, col),
                device_id_type=MESH,
            ).start()

        @pl.when(is_last & (target == SEGS - 1))
        def _():
            pltpu.make_async_copy(held.at[m], fin.at[place], fin_sem.at[place]).start()

    pl.when(is_first)(lambda: load_first(0))

    tiles_copy.wait()
    for j in range(CAP):
        weights[j] = raw[order_ref[j]]
    sums[CAP] = jnp.zeros((PAD, TB), F32)
    bias_copy.wait()

    @pl.when(is_first)
    def _():
        for m in range(1, AHEAD):
            load_first(m)

    if RELAY:
        pl.when(jnp.logical_not(is_first))(lambda: relay(0))

    def step(m, carry):
        pl.when(is_first & (m + AHEAD < MICRO))(lambda: load_first(m + AHEAD))
        if RELAY:
            pl.when(jnp.logical_not(is_first) & (m + 1 < MICRO))(lambda: relay(m + 1))
        await_input(m)
        compute(m)
        send(m)
        return carry

    lax.fori_loop(0, MICRO, step, 0)

    for place in range(FIN):
        pltpu.make_async_copy(fin.at[place], fin.at[place], fin_sem.at[place]).wait()
        for c in range(OWN):
            out_ref[place * R:(place + 1) * R, c * TB:(c + 1) * TB] = fin[place, c:c + 1]

    def drain(part, sem):
        pltpu.make_async_copy(part, part, send_sem.at[sem]).wait()

    half_shape = held.at[:, pl.ds(0, REACH)]

    @pl.when(is_last)
    def _():
        drain(held.at[pl.ds(0, MICRO - FIN)], 0)

    @pl.when(jnp.logical_not(is_last))
    def _():
        drain(held, 0)
        pl.when(has_far)(lambda: drain(half_shape, 1))
        if not RELAY:
            drain(half_shape, 2)

    if RELAY:
        pl.when(jnp.logical_not(is_first))(lambda: drain(half_shape, 2))

    @pl.when(is_first)
    def _():
        pl.when(has_far)(lambda: drain(half_shape, 3))
        drain(half_shape, 4)


def prepare(tile_row, tile_col, tile_count):
    column = lax.axis_index("col")
    slots = jnp.arange(CAP, dtype=jnp.int32)
    valid = slots < tile_count[0, 0]
    row = jnp.where(valid, tile_row[0] - column * OWN + REACH, REACH)
    target = jnp.where(valid, tile_col[0], OWN)
    key = target * CAP + slots
    rank = jnp.sum((key[None, :] < key[:, None]).astype(jnp.int32), axis=1)
    place = rank[None, :] == slots[:, None]

    def ordered(values):
        return jnp.sum(jnp.where(place, values[None, :], 0), axis=1)

    order, row, target_sorted = ordered(slots), ordered(row), ordered(target)
    former = jnp.concatenate([jnp.full((1,), -1, jnp.int32), target_sorted[:-1]])
    same = (target_sorted == former).astype(jnp.int32)
    blocks = jnp.arange(OWN, dtype=jnp.int32)
    count = jnp.sum((target[None, :] == blocks[:, None]).astype(jnp.int32), axis=1)
    upto = jnp.sum((target[None, :] <= blocks[:, None]).astype(jnp.int32), axis=1)
    last = jnp.where(count > 0, upto - 1, CAP)
    return order, row, same, last


def local(acts, tiles, tile_row, tile_col, tile_count, bias):
    tables = prepare(tile_row, tile_col, tile_count)
    smem = pl.BlockSpec(memory_space=pltpu.SMEM)
    vmem = pl.BlockSpec(memory_space=pltpu.VMEM)
    hbm = pl.BlockSpec(memory_space=pl.ANY)
    dma = pltpu.SemaphoreType.DMA
    return pl.pallas_call(
        kernel,
        out_shape=jax.ShapeDtypeStruct((ROWS // SEGS, OWN * TB), F32),
        in_specs=[smem, smem, smem, smem, hbm, hbm, hbm],
        out_specs=vmem,
        scratch_shapes=[
            pltpu.VMEM((ROWS // 8, 8, OWN * TB), F32),
            pltpu.VMEM((CAP, TB, TB), BF16),
            pltpu.VMEM((CAP, TB, TB), BF16),
            pltpu.VMEM((OWN, TB), F32),
            pltpu.VMEM((MICRO, EXT, TB), F32),
            pltpu.VMEM((MICRO, OWN, TB), F32),
            pltpu.VMEM((EXT, TB), F32),
            pltpu.VMEM((CAP + 1, PAD, TB), F32),
            pltpu.VMEM((OWN * PAD, TB), F32),
            pltpu.VMEM((FIN, OWN, TB), F32),
            dma((MICRO, 2)),
            dma((MICRO, 2)),
            dma((FIN,)),
            dma((5,)),
            dma((3,)),
        ],
        compiler_params=pltpu.CompilerParams(
            collective_id=0, has_side_effects=True, vmem_limit_bytes=60 << 20
        ),
        cost_estimate=pl.CostEstimate(
            flops=2 * ROWS * CAP * TB * TB, bytes_accessed=8 << 20, transcendentals=0
        ),
    )(*tables, acts.reshape(ROWS // 8, 8, OWN * TB), tiles[0], bias.reshape(OWN, TB))


def solution(mesh):
    placed = (
        P(None, "col"),
        P("segment", "col", None, None),
        P("segment", "col"),
        P("segment", "col"),
        P("segment", "col"),
        P("segment", "col"),
    )
    return jax.shard_map(
        local, mesh=mesh, in_specs=placed, out_specs=P("segment", "col"), check_vma=False
    )
```
